32 devices in a mesh: dp: 4 (over y, x), seq: 8 (over z, core).
Axes of the slice: x: 2, y: 2, z: 4, core: 2. Of those that a mesh axis runs over, the one named last changes fastest.
Arguments:
- tokens: bfloat16 [8, 1280, 2048], P('dp', 'seq'), may hold values from -6 to 6
- cotangent: bfloat16 [8, 1280, 2048], P('dp', 'seq'), may hold values from -6 to 6
- lengths: int32 [8], P('dp'), may hold values from 320 to 1280, as said below
- gain_master: float32 [2, 2048], P(None, ('dp', 'seq')), may hold values from 0.5 to 7, as said below
- gain_first: float32 [2, 2048], P(None, ('dp', 'seq')), may hold values from -0.0008544922 to 0.0008544922
- gain_second: float32 [2, 2048], P(None, ('dp', 'seq')), may hold values from 3.567091e-09 to 4.458864e-08
- vector_master: float32 [8, 2816], P(None, ('dp', 'seq')), may hold values from -20 to 2.5, as said below
- vector_first: float32 [8, 2816], P(None, ('dp', 'seq')), may hold values from -0.0008544922 to 0.0008544922
- vector_second: float32 [8, 2816], P(None, ('dp', 'seq')), may hold values from 3.567091e-09 to 4.458864e-08
- gate_master: float32 [2816, 2, 176], P(('dp', 'seq')), may hold values from -0.4375 to 0.4375
- gate_first: float32 [2816, 2, 176], P(('dp', 'seq')), may hold values from -0.0008544922 to 0.0008544922
- gate_second: float32 [2816, 2, 176], P(('dp', 'seq')), may hold values from 3.567091e-09 to 4.458864e-08
- temporal_master: float32 [2048, 3, 2816], P(('dp', 'seq')), may hold values from -0.125 to 0.125
- temporal_first: float32 [2048, 3, 2816], P(('dp', 'seq')), may hold values from -0.0008544922 to 0.0008544922
- temporal_second: float32 [2048, 3, 2816], P(('dp', 'seq')), may hold values from 3.567091e-09 to 4.458864e-08
- mlp_master: float32 [2048, 3, 6144], P(('dp', 'seq')), may hold values from -0.125 to 0.125
- mlp_first: float32 [2048, 3, 6144], P(('dp', 'seq')), may hold values from -0.0008544922 to 0.0008544922
- mlp_second: float32 [2048, 3, 6144], P(('dp', 'seq')), may hold values from 3.567091e-09 to 4.458864e-08
Outputs:
- block_out: bfloat16 [8, 1280, 2048], P('dp', 'seq')
- tokens_grad: bfloat16 [8, 1280, 2048], P('dp', 'seq')
- grad_norm: float32 [], replicated
- gain_new: float32 [2, 2048], P(None, ('dp', 'seq'))
- gain_first_new: float32 [2, 2048], P(None, ('dp', 'seq'))
- gain_second_new: float32 [2, 2048], P(None, ('dp', 'seq'))
- gain_copy: bfloat16 [2, 2048], P(None, ('dp', 'seq'))
- vector_new: float32 [8, 2816], P(None, ('dp', 'seq'))
- vector_first_new: float32 [8, 2816], P(None, ('dp', 'seq'))
- vector_second_new: float32 [8, 2816], P(None, ('dp', 'seq'))
- vector_copy: bfloat16 [8, 2816], P(None, ('dp', 'seq'))
- gate_new: float32 [2816, 2, 176], P(('dp', 'seq'))
- gate_first_new: float32 [2816, 2, 176], P(('dp', 'seq'))
- gate_second_new: float32 [2816, 2, 176], P(('dp', 'seq'))
- gate_copy: bfloat16 [2816, 2, 176], P(('dp', 'seq'))
- temporal_new: float32 [2048, 3, 2816], P(('dp', 'seq'))
- temporal_first_new: float32 [2048, 3, 2816], P(('dp', 'seq'))
- temporal_second_new: float32 [2048, 3, 2816], P(('dp', 'seq'))
- temporal_copy: bfloat16 [2048, 3, 2816], P(('dp', 'seq'))
- mlp_new: float32 [2048, 3, 6144], P(('dp', 'seq'))
- mlp_first_new: float32 [2048, 3, 6144], P(('dp', 'seq'))
- mlp_second_new: float32 [2048, 3, 6144], P(('dp', 'seq'))
- mlp_copy: bfloat16 [2048, 3, 6144], P(('dp', 'seq'))
The draws below stay inside these ranges and needn't reach their ends.
Inputs may be any that keep to these rules, and one draw needn't show every extreme that they name: `lengths`: among the 2 sequences of each index of dp one has length exactly 1280; positions at or past a length are padding. `gain_master`: positive gains. `vector_master`: row 7 is negative.
All inputs are finite; a program needn't handle non-finite values.
Results may differ from the reference program's by a relative error of at most 0.035.
Values may be sent and summed in bfloat16 or wider, within the bound.
A program may use at most 768 MiB of HBM per device.

```python
import math
import jax
import jax.numpy as jnp
from jax import lax

D = 2048
R = 2816
FF = 6144
NB = 16
BS = 176
SEQS = 2
STEP = 10
SEQ_LEN = 1280
NSEQ_ALL = 8
NPARAM = 56068096


def draw_lengths(key, part):
    key = jax.random.fold_in(key, 13)
    first_key, second_key = jax.random.split(key)
    groups = NSEQ_ALL // SEQS
    drawn_lengths = jax.random.randint(first_key, (groups, SEQS), SEQ_LEN // 4, SEQ_LEN + 1)
    chosen = jax.random.randint(second_key, (groups, 1), 0, SEQS)
    slot_ids = jnp.arange(SEQS, dtype=jnp.int32)[None, :]
    return jnp.where(slot_ids == chosen, SEQ_LEN, drawn_lengths).reshape(NSEQ_ALL).astype(jnp.int32)


def draw_gain_master(key, part):
    key = jax.random.fold_in(key, 11)
    ramp = jnp.arange(D, dtype=jnp.float32) / D
    noise = jnp.clip(1.0 + 0.15 * jax.random.normal(key, (2, D), jnp.float32), 0.55, 1.45)
    values = (1.0 + 2.0 * ramp)[None, :] * noise
    return values.astype(jnp.float32)


def draw_vector_master(key, part):
    key = jax.random.fold_in(key, 12)
    subkeys = jax.random.split(key, 3)
    conv_taps = jnp.clip(0.5 * jax.random.normal(subkeys[0], (5, R), jnp.float32), -2.5, 2.5)
    biases = jnp.clip(0.7 * jax.random.normal(subkeys[1], (2, R), jnp.float32), -2.5, 2.5)
    decay_rates = jnp.exp(jax.random.uniform(subkeys[2], (1, R), jnp.float32, math.log(0.5 / SEQ_LEN), math.log(1.0 / 30.0)))
    softplus_target = decay_rates / 4.0
    lam_raw = jnp.log(jnp.expm1(softplus_target))
    return jnp.concatenate([conv_taps, biases, lam_raw], axis=0).astype(jnp.float32)


def steps_of(stream_key, extent, cuts, low, high):
    gain = 1.0
    for position, parts in cuts:
        heights = jax.random.uniform(jax.random.fold_in(jax.random.fold_in(stream_key, 6), position), (parts,), jnp.float32, low / len(cuts), high / len(cuts))
        gain = gain * jnp.repeat(jnp.exp(heights), extent[position] // parts).reshape((-1,) + (1,) * (len(extent) - 1 - position))
    return gain


def centred(key, dims, width, bound, pieces=(), kind=jnp.bfloat16):
    drawn = jax.random.normal(key, dims, jnp.float32) * width
    if len(pieces) > 0:
        drawn = steps_of(key, dims, pieces, -0.22, 0.18) * drawn
    return jnp.clip(drawn, min=-bound, max=bound).astype(kind)


def setup_inputs(seed: int = 0) -> dict:
    key_list = jax.random.split(jax.random.key(seed), 19)
    return {
        "tokens": centred(key_list[0], (NSEQ_ALL, SEQ_LEN, D), 1.0, 6.0, ((0, 4), (1, 8))),
        "cotangent": centred(key_list[1], (NSEQ_ALL, SEQ_LEN, D), 1.0, 6.0, ((0, 4), (1, 8))),
        "lengths": draw_lengths(jax.random.fold_in(key_list[18], 71), 0),
        "gain_master": draw_gain_master(jax.random.fold_in(key_list[18], 71), 0),
        "gain_first": centred(key_list[4], (2, D), (NPARAM ** -0.5), 0.0008544922, ((1, 32),), jnp.float32),
        "gain_second": jnp.clip(jnp.exp(math.log(4.4588638559162064e-08) - 2.5257286 * jax.random.uniform(key_list[5], (2, D), jnp.float32) ** steps_of(key_list[5], (2, D), ((1, 32),), -0.2, 0.2)), 3.5670910669693967e-09, 4.4588638559162064e-08),
        "vector_master": draw_vector_master(jax.random.fold_in(key_list[18], 71), 0),
        "vector_first": centred(key_list[7], (8, R), (NPARAM ** -0.5), 0.0008544922, ((1, 32),), jnp.float32),
        "vector_second": jnp.clip(jnp.exp(math.log(4.4588638559162064e-08) - 2.5257286 * jax.random.uniform(key_list[8], (8, R), jnp.float32) ** steps_of(key_list[8], (8, R), ((1, 32),), -0.2, 0.2)), 3.5670910669693967e-09, 4.4588638559162064e-08),
        "gate_master": centred(key_list[9], (R, 2, BS), BS ** -0.5, 0.4375, ((0, 32),), jnp.float32),
        "gate_first": centred(key_list[10], (R, 2, BS), (NPARAM ** -0.5), 0.0008544922, ((0, 32),), jnp.float32),
        "gate_second": jnp.clip(jnp.exp(math.log(4.4588638559162064e-08) - 2.5257286 * jax.random.uniform(key_list[11], (R, 2, BS), jnp.float32) ** steps_of(key_list[11], (R, 2, BS), ((0, 32),), -0.2, 0.2)), 3.5670910669693967e-09, 4.4588638559162064e-08),
        "temporal_master": centred(key_list[12], (D, 3, R), D ** -0.5, 0.125, ((0, 32),), jnp.float32),
        "temporal_first": centred(key_list[13], (D, 3, R), (NPARAM ** -0.5), 0.0008544922, ((0, 32),), jnp.float32),
        "temporal_second": jnp.clip(jnp.exp(math.log(4.4588638559162064e-08) - 2.5257286 * jax.random.uniform(key_list[14], (D, 3, R), jnp.float32) ** steps_of(key_list[14], (D, 3, R), ((0, 32),), -0.2, 0.2)), 3.5670910669693967e-09, 4.4588638559162064e-08),
        "mlp_master": centred(key_list[15], (D, 3, FF), D ** -0.5, 0.125, ((0, 32),), jnp.float32),
        "mlp_first": centred(key_list[16], (D, 3, FF), (NPARAM ** -0.5), 0.0008544922, ((0, 32),), jnp.float32),
        "mlp_second": jnp.clip(jnp.exp(math.log(4.4588638559162064e-08) - 2.5257286 * jax.random.uniform(key_list[17], (D, 3, FF), jnp.float32) ** steps_of(key_list[17], (D, 3, FF), ((0, 32),), -0.2, 0.2)), 3.5670910669693967e-09, 4.4588638559162064e-08),
    }


@jax.custom_vjp
def low(v):
    return lax.optimization_barrier(v.astype(jnp.bfloat16)).astype(jnp.float32)

@jax.custom_vjp
def low_back(v):
    return v

def low_keep(v):
    return (low(v), None)

def low_pass(kept, grad):
    return (grad,)

def back_keep(v):
    return (v, None)

def back_low(kept, grad):
    return (low(grad),)
low.defvjp(low_keep, low_pass)
low_back.defvjp(back_keep, back_low)
NORM_EPS = 1e-06
GATE_SCALE = 8.0
BETA_ONE = 0.5
BETA_TWO = 0.75
ADAM_EPS = 1e-08
WEIGHT_DECAY = 0.1
CLIP_LEVEL = 1.0

def exact_dot(left_side, right_side):
    return jnp.dot(left_side, right_side, precision=lax.Precision.HIGHEST)

def rms_norm(values, gain_vec):
    return values * lax.rsqrt(lax.optimization_barrier(jnp.mean(values * values, axis=-1, keepdims=True)) + NORM_EPS) * gain_vec

def combine_pair(earlier, later_pair):
    return (earlier[0] + later_pair[0], jnp.exp(later_pair[0]) * earlier[1] + later_pair[1])

def gate_piece(gated_all, conv_out, bias_recur, bias_inner, lam_raw):
    recur_gate = jax.nn.sigmoid(gated_all[:, 0] + bias_recur)
    inner_gate = jax.nn.sigmoid(gated_all[:, 1] + bias_inner)
    log_decay = -GATE_SCALE * jax.nn.softplus(lam_raw) * recur_gate
    driven = jnp.sqrt(-jnp.expm1(2.0 * log_decay)) * (inner_gate * conv_out)
    return (log_decay, driven)

def one_sequence(params, seq_rows):
    gain_rows, vectors, gate_pack, temporal, mlp_pack = params
    length = seq_rows.shape[0]
    inner_width = temporal.shape[2]
    block_size = inner_width // NB
    normed_one = low(rms_norm(seq_rows, gain_rows[0]))
    conv_input = low(low_back(exact_dot(normed_one, temporal[:, 0, :])))
    gate_branch = low_back(exact_dot(normed_one, temporal[:, 1, :]))
    gate_act = jax.nn.gelu(gate_branch, approximate=True)
    padded = jnp.concatenate([jnp.zeros((3, inner_width), jnp.float32), conv_input], axis=0)
    conv_sum = vectors[4] + sum((vectors[offset] * padded[3 - offset:3 - offset + length] for offset in range(4)))
    conv_out = low(low_back(conv_sum))
    blocks = conv_out.reshape(length, NB, block_size)
    gated_all = jnp.einsum('tbi,bikj->tbkj', blocks, gate_pack.reshape(NB, block_size, 2, block_size), precision=lax.Precision.HIGHEST)
    gated_all = low_back(jnp.transpose(gated_all, (0, 2, 1, 3)).reshape(length, 2, inner_width))
    log_decay, driven = gate_piece(gated_all, conv_out, vectors[5], vectors[6], vectors[7])
    _, full_state = lax.associative_scan(combine_pair, (log_decay, driven), axis=0)
    mixed_out = low(full_state * gate_act)
    residual_one = seq_rows + low_back(exact_dot(mixed_out, temporal[:, 2, :].T))
    normed_two = low(rms_norm(residual_one, gain_rows[1]))
    gate_mlp = low_back(exact_dot(normed_two, mlp_pack[:, 0, :]))
    up_mlp = low_back(exact_dot(normed_two, mlp_pack[:, 1, :]))
    hidden = low(jax.nn.gelu(gate_mlp, approximate=True) * up_mlp)
    return residual_one + low_back(exact_dot(hidden, mlp_pack[:, 2, :].T))

def adam_update(weight, first_moment, second, gradient, step_rate, decay_rate):
    first_new = BETA_ONE * first_moment + (1.0 - BETA_ONE) * gradient
    second_new = BETA_TWO * second + (1.0 - BETA_TWO) * gradient * gradient
    adam_step = first_new / (1.0 - BETA_ONE ** STEP) / (jnp.sqrt(second_new / (1.0 - BETA_TWO ** STEP)) + ADAM_EPS)
    weight_new = weight - step_rate * (adam_step + decay_rate * weight)
    return (weight_new, first_new, second_new, weight_new.astype(jnp.bfloat16))

def reference(tokens, cotangent, lengths, gain_master, gain_first, gain_second, vector_master, vector_first, vector_second, gate_master, gate_first, gate_second, temporal_master, temporal_first, temporal_second, mlp_master, mlp_first, mlp_second):
    masters = (gain_master, vector_master, gate_master, temporal_master, mlp_master)
    params = tuple((weight.astype(jnp.bfloat16).astype(jnp.float32) for weight in masters))
    inputs = tokens.astype(jnp.float32)
    positions = jnp.arange(SEQ_LEN, dtype=jnp.int32)
    is_valid = (positions[None, :] < lengths[:, None]).astype(jnp.float32)

    def forward(weights, token_rows):
        return lax.map(jax.checkpoint(lambda sequence: one_sequence(weights, sequence)), token_rows)
    outputs, pullback = jax.vjp(forward, params, inputs)
    gradients, input_grad = pullback(cotangent.astype(jnp.float32) * is_valid[:, :, None])
    squares = sum((jnp.sum(grad_part * grad_part) for grad_part in gradients))
    grad_norm = jnp.sqrt(squares)
    factor = CLIP_LEVEL / jnp.maximum(grad_norm, CLIP_LEVEL)
    block_size = R // NB
    gain_out = adam_update(gain_master, gain_first, gain_second, gradients[0] * factor, 1.0, 0.0)
    vector_out = adam_update(vector_master, vector_first, vector_second, gradients[1] * factor, 2.0, 0.0)
    gate_out = adam_update(gate_master, gate_first, gate_second, gradients[2] * factor, block_size ** (-0.5), WEIGHT_DECAY)
    temporal_out = adam_update(temporal_master, temporal_first, temporal_second, gradients[3] * factor, D ** (-0.5), WEIGHT_DECAY)
    mlp_out = adam_update(mlp_master, mlp_first, mlp_second, gradients[4] * factor, D ** (-0.5), WEIGHT_DECAY)
    return (outputs.astype(jnp.bfloat16), input_grad.astype(jnp.bfloat16), grad_norm, gain_out[0], gain_out[1], gain_out[2], gain_out[3], vector_out[0], vector_out[1], vector_out[2], vector_out[3], gate_out[0], gate_out[1], gate_out[2], gate_out[3], temporal_out[0], temporal_out[1], temporal_out[2], temporal_out[3], mlp_out[0], mlp_out[1], mlp_out[2], mlp_out[3])
```

```python
import functools
import math

import jax
import jax.numpy as jnp
from jax import lax
from jax.experimental import pallas as pl
from jax.experimental.pallas import tpu as pltpu
from jax.sharding import PartitionSpec as P

NB = 16
STEP = 10
NORM_EPS = 1e-06
GATE_SCALE = 8.0
BETA_ONE = 0.5
BETA_TWO = 0.75
ADAM_EPS = 1e-08
WEIGHT_DECAY = 0.1
CLIP_LEVEL = 1.0
GELU_SCALE = math.sqrt(2.0 / math.pi)
GELU_CUBE = 0.044715
LANES = 128
MIB = 1024 * 1024
MESH = pl.DeviceIdType.MESH
F32 = jnp.float32
BF16 = jnp.bfloat16


def dot(a, b, ca=1, cb=0):
    return lax.dot_general(a, b, (((ca,), (cb,)), ((), ())), preferred_element_type=F32)


def dp_peers():
    me = lax.axis_index("dp")
    return me + 1 - 2 * (me % 2), (me + 2) % 4


def meet(peers):
    barrier = pltpu.get_barrier_semaphore()
    for peer in peers:
        pl.semaphore_signal(barrier, inc=1, device_id=peer, device_id_type=MESH)
    pl.semaphore_wait(barrier, len(peers))


def dp_sender(send_sem, recv_sem):
    seq = lax.axis_index("seq")

    def send(k, src, dst, peer):
        copy = pltpu.make_async_remote_copy(
            src, dst, send_sem.at[k], recv_sem.at[k], device_id=(peer, seq), device_id_type=MESH
        )
        copy.start()
        return copy

    return send


def gather_start(send, k, src, o, one, two):
    half = src.shape[0] // 2
    first, second = pl.ds(0, half), pl.ds(half, half)
    return [
        send(k, src.at[first], o.at[1, first], one),
        send(k + 1, src.at[second], o.at[2, second], two),
        send(k + 2, src.at[second], o.at[1, second], one),
        send(k + 3, src.at[first], o.at[2, first], two),
    ]


def gather_forward(send, k, near, o, one, two):
    half = o.shape[1] // 2
    first, second = pl.ds(0, half), pl.ds(half, half)
    near[0].wait_recv()
    far = [send(k + 4, o.at[1, first], o.at[3, first], two)]
    near[1].wait_recv()
    far.append(send(k + 5, o.at[2, second], o.at[3, second], one))
    return far


def gather_wait(near, far):
    near[2].wait_recv()
    near[3].wait_recv()
    for copy in far:
        copy.wait_recv()
    for copy in near + far:
        copy.wait_send()


def gather_end(send, k, near, o, one, two):
    gather_wait(near, gather_forward(send, k, near, o, one, two))


def starter(send_sem, recv_sem):
    def send(k, src, dst, peer):
        copy = pltpu.make_async_remote_copy(
            src, dst, send_sem.at[k], recv_sem.at[k], device_id=peer, device_id_type=MESH
        )
        copy.start()
        return copy

    return send


def dp_others():
    me, seq = lax.axis_index("dp"), lax.axis_index("seq")
    one, two = dp_peers()
    return [(3 - me, seq), (one, seq), (two, seq)]


def columns_start(send, k, buf, outs, own_sem):
    me = lax.axis_index("dp")
    copies, first = [], 0
    for out in outs:
        at = pl.ds(first, out.shape[2])
        for peer in dp_others():
            copies.append(send(k, buf.at[peer[0], :, at], out.at[me], peer))
            k += 1
        first += out.shape[2]
    own, first = [], 0
    for j, out in enumerate(outs):
        at = pl.ds(first, out.shape[2])
        own.append(pltpu.make_async_copy(buf.at[me, :, at], out.at[me], own_sem.at[j]))
        own[-1].start()
        first += out.shape[2]
    return copies + own


def owners_start(send, k, pairs, own_sem):
    me = lax.axis_index("dp")
    copies = []
    for j, (src, out) in enumerate(pairs):
        depth = out.shape[1]

        def rows(dp):
            at = pl.ds(pl.multiple_of(dp * depth, 16), depth)
            return src.at[at, pl.ds(0, out.shape[2])]

        for peer in dp_others():
            copies.append(send(k, rows(peer[0]), out.at[me], peer))
            k += 1
        copies.append(pltpu.make_async_copy(rows(me), out.at[me], own_sem.at[j]))
        copies[-1].start()
    return copies


def fill_columns(w, buf):
    depth, cols = w.shape[1], w.shape[2] // 4
    spare = buf.shape[2] - 3 * cols
    for dp in range(4):
        pieces = [w[k, :, dp * cols : (dp + 1) * cols] for k in range(3)]
        if spare:
            pieces.append(jnp.zeros((depth, spare), F32))
        buf[dp] = jnp.concatenate(pieces, axis=1).astype(BF16)


def temporal_front_body(
    count,
    w,
    gates_s,
    vec_s,
    gains_s,
    t_o,
    gates_o,
    vec_o,
    gains_o,
    buf,
    gates,
    vec,
    gains,
    over,
    own_sem,
    send_sem,
    recv_sem,
):
    dp, me = lax.axis_index("dp"), lax.axis_index("seq")
    line = [(dp, (me + 2 * j) % count) for j in range(1, count // 2)]
    other = (dp, me + 1 - 2 * (me % 2))
    meet(dp_others() + line + [other])
    send = starter(send_sem, recv_sem)
    share, _, size = gates_s.shape
    for ref in (gates, vec, gains):
        ref[...] = jnp.zeros_like(ref)
    vec[:, 0:share] = vec_s[...].astype(BF16).astype(F32)
    gains[0:2, 0 : gains_s.shape[1]] = gains_s[...].astype(BF16).astype(F32)
    early = [send(3 + k, gains, over.at[dp], peer) for k, peer in enumerate(dp_others())]
    fill_columns(w, buf)
    columns = columns_start(send, 0, buf, [t_o], own_sem)
    for k in range(2):
        gates[0:share, k * size : (k + 1) * size] = gates_s[:, k, :].astype(BF16)
    gates_o[me] = gates[...]
    vec_o[me] = vec[...]
    over[dp] = gains[...]
    outs = (gates_o, vec_o, gains_o)
    core = 6 + 3 * len(line)
    small = []

    def along(part, src):
        got = [send(6 + 3 * j + part, src, outs[part].at[me], peer) for j, peer in enumerate(line)]
        small.append(send(core + part, src, outs[part].at[me], other))
        return got

    arriving = [along(0, gates), along(1, vec)]
    for copy in early:
        copy.wait()
    gains_o[me] = over[...]
    arriving.append(along(2, over))
    for j in range(len(line)):
        index = (me - 2 * (j + 1) + count) % count
        for part, out in enumerate(outs):
            arriving[part][j].wait_recv()
            small.append(send(core + 3 * (j + 1) + part, out.at[index], out.at[index], other))
    for copy in arriving[0] + arriving[1] + arriving[2]:
        copy.wait_send()
    for copy in columns + small:
        copy.wait()


def temporal_front(w, width, gates, vec, gains):
    count = lax.axis_size("seq")
    depth = w.shape[1]
    share, _, size = gates.shape
    gate_tile = (-(-share // 16) * 16, -(-2 * size // LANES) * LANES)
    small = (8, LANES)
    vmem = pl.BlockSpec(memory_space=pltpu.VMEM)
    sems = 6 + 3 * (count - 1)
    return pl.pallas_call(
        functools.partial(temporal_front_body, count),
        out_shape=(
            jax.ShapeDtypeStruct((4, depth, width), BF16),
            jax.ShapeDtypeStruct((count,) + gate_tile, BF16),
            jax.ShapeDtypeStruct((count,) + small, F32),
            jax.ShapeDtypeStruct((count, 4) + small, F32),
        ),
        in_specs=[vmem] * 4,
        out_specs=(pl.BlockSpec(memory_space=pl.ANY),) + (vmem,) * 3,
        scratch_shapes=[
            pltpu.VMEM((4, depth, width), BF16),
            pltpu.VMEM(gate_tile, BF16),
            pltpu.VMEM(small, F32),
            pltpu.VMEM(small, F32),
            pltpu.VMEM((4,) + small, F32),
            pltpu.SemaphoreType.DMA((1,)),
            pltpu.SemaphoreType.DMA((sems,)),
            pltpu.SemaphoreType.DMA((sems,)),
        ],
        compiler_params=pltpu.CompilerParams(
            collective_id=0, has_side_effects=True, vmem_limit_bytes=60 * MIB
        ),
        name="temporal_front",
    )(w, gates, vec, gains)


def front_body(
    count,
    nb,
    size,
    share,
    depth,
    order,
    w,
    x_s,
    gates_all,
    vec_all,
    gains_all,
    tile,
    gu_o,
    d_o,
    n_o,
    mix_o,
    vec_o,
    lam_o,
    gain_o,
    x_o,
    buf,
    x,
    x_all,
    gates_full,
    own_sem,
    send_sem,
    recv_sem,
):
    dp, me = lax.axis_index("dp"), lax.axis_index("seq")
    one, two = dp_peers()
    along = [(dp, (me + j) % count) for j in range(1, count)]
    meet(dp_others() + along)
    send = starter(send_sem, recv_sem)
    rows, wide = x.shape
    half = rows // 2
    first, second = pl.ds(0, half), pl.ds(half, half)
    part = wide // len(order)
    raw = x_s[...]
    x[...] = jnp.concatenate([raw[:, b * part : (b + 1) * part] for b in order], axis=1)
    x_o[...] = x[...]
    near = [
        send(0, x.at[first], x_all.at[1, first], (one, me)),
        send(1, x.at[second], x_all.at[2, second], (two, me)),
        send(2, x.at[second], x_all.at[1, second], (one, me)),
        send(3, x.at[first], x_all.at[2, first], (two, me)),
    ]
    fill_columns(w, buf)
    near[0].wait_recv()
    far = [send(4, x_all.at[1, first], x_all.at[3, first], (two, me))]
    near[1].wait_recv()
    far.append(send(5, x_all.at[2, second], x_all.at[3, second], (one, me)))
    columns = columns_start(send, 6, buf, [gu_o, d_o], own_sem)

    pieces = [gains_all[p, k, :, 0:depth] for p in range(count) for k in range(4)]
    gain_o[...] = jnp.concatenate(pieces, axis=1)
    width = vec_o.shape[1]
    used = nb * size
    pieces = [vec_all[p, :, 0:share] for p in range(count)]
    vectors = jnp.concatenate(pieces + [jnp.zeros((8, width - used), F32)], axis=1)
    vec_o[...] = vectors
    lam = vectors[7:8]
    lam_o[...] = jnp.broadcast_to(lam, lam_o.shape)
    vec_o[7:8] = -GATE_SCALE * softplus(lam)
    for p in range(count):
        gates_full[p * share : (p + 1) * share] = gates_all[p, 0:share].astype(F32)
    mix_o[...] = jnp.zeros_like(mix_o)
    for k in range(2):
        for b in range(nb):
            at = slice(b * size, (b + 1) * size)
            block = gates_full[at, k * size : (k + 1) * size].astype(BF16)
            spread = dot(block, tile[...])
            column = lax.broadcasted_iota(jnp.int32, spread.shape, 1)
            inside = (column >= b * size) & (column < (b + 1) * size)
            mix_o[at, k * width : k * width + used] = jnp.where(inside, spread, 0.0).astype(BF16)
    step = 32

    def norm(src, k):
        def piece(j, c):
            r = pl.ds(pl.multiple_of(j * step, step), step)
            v = (x[r] if src is None else x_all[src, r]).astype(F32)
            to = pl.ds(pl.multiple_of(k * rows + j * step, step), step)
            n_o[to] = (v * inverse_rms(v) * gain_o[0:1]).astype(BF16)
            return c

        lax.fori_loop(0, rows // step, piece, 0)

    norm(None, 0)
    near[2].wait_recv()
    norm(1, 1)
    near[3].wait_recv()
    norm(2, 2)
    for copy in far:
        copy.wait_recv()
    norm(3, 3)
    for copy in near + far:
        copy.wait_send()
    for copy in columns:
        copy.wait()


def front(w, x, gates, vec, gains, share, size, nb, width, order):
    count = lax.axis_size("seq")
    rows, wide = x.shape
    cols = w.shape[2] // 4
    depth = w.shape[1]
    tile = jnp.tile(jnp.eye(size, dtype=BF16), (1, nb))
    vmem = pl.BlockSpec(memory_space=pltpu.VMEM)
    anywhere = pl.BlockSpec(memory_space=pl.ANY)
    sems = 12
    return pl.pallas_call(
        functools.partial(front_body, count, nb, size, share, depth, order),
        out_shape=(
            jax.ShapeDtypeStruct((4, depth, 2 * cols), BF16),
            jax.ShapeDtypeStruct((4, depth, cols), BF16),
            jax.ShapeDtypeStruct((4 * rows, wide), BF16),
            jax.ShapeDtypeStruct((width, 2 * width), BF16),
            jax.ShapeDtypeStruct((8, width), F32),
            jax.ShapeDtypeStruct((8, width), F32),
            jax.ShapeDtypeStruct((8, wide), F32),
            jax.ShapeDtypeStruct((rows, wide), BF16),
        ),
        in_specs=[vmem] * 6,
        out_specs=(anywhere, anywhere) + (vmem,) * 6,
        scratch_shapes=[
            pltpu.VMEM((4, depth, 3 * cols), BF16),
            pltpu.VMEM((rows, wide), BF16),
            pltpu.VMEM((4, rows, wide), BF16),
            pltpu.VMEM((nb * size, gates.shape[2]), F32),
            pltpu.SemaphoreType.DMA((2,)),
            pltpu.SemaphoreType.DMA((sems,)),
            pltpu.SemaphoreType.DMA((sems,)),
        ],
        compiler_params=pltpu.CompilerParams(
            collective_id=6, has_side_effects=True, vmem_limit_bytes=60 * MIB
        ),
        name="front",
    )(w, x, gates, vec, gains, tile)


def swap(v, k):
    return lax.ppermute(v, "dp", [(i, i ^ k) for i in range(4)])


def sum_swapped(parts):
    total = parts[0].astype(F32)
    for k in (3, 1, 2):
        total = total + swap(parts[k], k).astype(F32)
    return total


def sum_over(send, scratch, one, two, produce, meanwhile=None):
    p, via_one, via_two, to_one, to_two, from_one, from_two = scratch
    half, step = via_one.shape[0], 16
    first, second = pl.ds(0, half), pl.ds(half, half)
    produce(3)
    copies = [
        send(0, p.at[3, first], via_two, two),
        send(1, p.at[3, second], via_one, one),
    ]
    produce(1)
    copies.append(send(2, p.at[1, second], from_one.at[second], one))
    produce(2)
    copies.append(send(3, p.at[2, first], from_two.at[first], two))
    copies[0].wait_recv()

    def add_two(k, c):
        r = pl.ds(pl.multiple_of(k * step, step), step)
        to_one[r] = (p[1, r].astype(F32) + via_two[r].astype(F32)).astype(BF16)
        return c

    lax.fori_loop(0, half // step, add_two, 0)
    copies.append(send(4, to_one, from_one.at[first], one))
    copies[1].wait_recv()

    def add_one(k, c):
        r = pl.ds(pl.multiple_of(k * step, step), step)
        q = pl.ds(pl.multiple_of(half + k * step, step), step)
        to_two[r] = (p[2, q].astype(F32) + via_one[r].astype(F32)).astype(BF16)
        return c

    lax.fori_loop(0, half // step, add_one, 0)
    copies.append(send(5, to_two, from_two.at[second], two))
    produce(0)
    if meanwhile is not None:
        meanwhile()
    for copy in copies[2:]:
        copy.wait_recv()
    return copies


def sum_scratch(rows, width):
    return [
        pltpu.VMEM((4, rows, width), BF16),
        pltpu.VMEM((rows // 2, width), BF16),
        pltpu.VMEM((rows // 2, width), BF16),
        pltpu.VMEM((rows // 2, width), BF16),
        pltpu.VMEM((rows // 2, width), BF16),
        pltpu.VMEM((rows, width), BF16),
        pltpu.VMEM((rows, width), BF16),
        pltpu.VMEM((rows, width), BF16),
        pltpu.SemaphoreType.DMA,
        pltpu.SemaphoreType.DMA((24,)),
        pltpu.SemaphoreType.DMA((24,)),
    ]


def sum_and_gather(produce, finish, out, scratch, meanwhile=None):
    p, via_one, via_two, to_one, to_two, from_one, from_two, own, own_sem, send_sem, recv_sem = scratch
    one, two = dp_peers()
    seq = lax.axis_index("seq")
    meet([(one, seq), (two, seq)])
    send = dp_sender(send_sem, recv_sem)
    step = 16
    block = own.shape[0] // 2
    half = block // 2
    copies, near, far = ([], []), [], []

    def halves(b):
        return pl.ds(b * block, half), pl.ds(b * block + half, half)

    def relays(b):
        first, second = halves(b)
        via = pl.ds(b * half, half)
        copies[b].append(send(12 * b, p.at[3, first], via_two.at[via], two))
        copies[b].append(send(12 * b + 1, p.at[3, second], via_one.at[via], one))

    def direct_one(b):
        second = halves(b)[1]
        copies[b].append(send(12 * b + 2, p.at[1, second], from_one.at[second], one))

    def direct_two(b):
        first = halves(b)[0]
        copies[b].append(send(12 * b + 3, p.at[2, first], from_two.at[first], two))

    def relay(b):
        first, second = halves(b)
        via = pl.ds(b * half, half)
        for j, (part, got, to, at) in enumerate(
            ((1, via_two, to_one, 0), (2, via_one, to_two, half))
        ):
            copies[b][j].wait_recv()

            def add(k, c):
                r = pl.ds(pl.multiple_of(b * half + k * step, step), step)
                q = pl.ds(pl.multiple_of(b * block + at + k * step, step), step)
                to[r] = (p[part, q].astype(F32) + got[r].astype(F32)).astype(BF16)
                return c

            lax.fori_loop(0, half // step, add, 0)
            if j == 0:
                copies[b].append(send(12 * b + 4, to_one.at[via], from_one.at[first], one))
            else:
                copies[b].append(send(12 * b + 5, to_two.at[via], from_two.at[second], two))

    def complete(b):
        for copy in copies[b][2:]:
            copy.wait_recv()

        def rows_of(k, c):
            r = pl.ds(pl.multiple_of(b * block + k * step, step), step)
            total = p[0, r].astype(F32) + from_one[r].astype(F32) + from_two[r].astype(F32)
            own[r] = finish(r, total).astype(BF16)
            return c

        lax.fori_loop(0, block // step, rows_of, 0)
        first, second = halves(b)
        k = 12 * b + 6
        near.append(
            [
                send(k, own.at[first], out.at[1, first], one),
                send(k + 1, own.at[second], out.at[2, second], two),
                send(k + 2, own.at[second], out.at[1, second], one),
                send(k + 3, own.at[first], out.at[2, first], two),
            ]
        )

    def forward(b):
        first, second = halves(b)
        near[b][0].wait_recv()
        far.append(send(12 * b + 10, out.at[1, first], out.at[3, first], two))
        near[b][1].wait_recv()
        far.append(send(12 * b + 11, out.at[2, second], out.at[3, second], one))

    produce(3)
    relays(0)
    produce(1)
    direct_one(0)
    produce(2)
    direct_two(0)
    relay(0)
    relays(1)
    direct_one(1)
    direct_two(1)
    produce(0)
    if meanwhile is not None:
        meanwhile()
    relay(1)
    complete(0)
    complete(1)
    keep = pltpu.make_async_copy(own, out.at[0], own_sem)
    keep.start()
    forward(0)
    forward(1)
    for b in range(2):
        near[b][2].wait_recv()
        near[b][3].wait_recv()
    for copy in far:
        copy.wait_recv()
    for copy in copies[0] + copies[1] + near[0] + near[1] + far:
        copy.wait_send()
    keep.wait()


def mid_body(span, first, h, y, w_t, x, gain, o_o, z_o, n_o, w_o, load_sem, *scratch):
    p = scratch[0]
    rows = x.shape[0]
    load = pltpu.make_async_copy(w_t.at[:, pl.ds(first, w_o.shape[1])], w_o, load_sem)
    load.start()
    load.wait()

    def produce(k):
        def piece(j, c):
            r = pl.ds(pl.multiple_of(k * rows + j * span, span), span)
            o = (h[r] * gelu(y[r])).astype(BF16)
            o_o[r] = o
            p[k, pl.ds(pl.multiple_of(j * span, span), span)] = dot(o, w_o[...], 1, 1).astype(BF16)
            return c

        lax.fori_loop(0, rows // span, piece, 0)

    def finish(r, total):
        z = x[r].astype(F32) + total
        z_o[r] = z
        return z * inverse_rms(z) * gain[...]

    sum_and_gather(produce, finish, n_o, scratch)


def mid(span, first, h, y, w_t, x, gain):
    rows, width = x.shape
    vmem = pl.BlockSpec(memory_space=pltpu.VMEM)
    return pl.pallas_call(
        functools.partial(mid_body, span, first),
        out_shape=(
            jax.ShapeDtypeStruct(h.shape, BF16),
            jax.ShapeDtypeStruct((rows, width), F32),
            jax.ShapeDtypeStruct((4, rows, width), BF16),
        ),
        in_specs=[vmem, vmem, pl.BlockSpec(memory_space=pl.ANY), vmem, vmem],
        out_specs=(vmem, vmem, pl.BlockSpec(memory_space=pl.ANY)),
        scratch_shapes=[pltpu.VMEM((width, h.shape[1]), BF16), pltpu.SemaphoreType.DMA]
        + sum_scratch(rows, width),
        compiler_params=pltpu.CompilerParams(
            collective_id=1, has_side_effects=True, vmem_limit_bytes=60 * MIB
        ),
        name="mid",
    )(h, y, w_t, x, gain)


def mlp_back_body(
    d_g, d_u, w_gu, hidden, w_d, z, d_out, gain, dz_o, dz_all, b0, b1, b2, b3, gu_v, w_v, load_sem, *scratch
):
    p = scratch[0]
    rows, width = z.shape
    tile = 256
    order = (3, 1, 2, 0)

    cols = d_g.shape[1]

    def load_rows(k, part=None):
        at = pl.ds(k * rows, rows)
        src, j = (d_g, 0) if part is None else (d_u, 1)
        to = gu_v.at[at, pl.ds(j * cols, cols)]
        return pltpu.make_async_copy(src.at[at], to, load_sem.at[4 * j + k])

    def load_tile(j):
        at = pl.ds(pl.multiple_of(j * tile, tile), tile)
        return pltpu.make_async_copy(w_gu.at[at], w_v.at[at], load_sem.at[8 + j])

    load_rows(3).start()
    load_rows(3, 1).start()
    for j in range(width // tile):
        load_tile(j).start()
    for k in order[1:]:
        load_rows(k).start()
        load_rows(k, 1).start()

    def produce(k):
        load_rows(k).wait()
        load_rows(k, 1).wait()

        def piece(j, c):
            if k == 3:
                load_tile(j).wait()
            at = pl.ds(pl.multiple_of(j * tile, tile), tile)
            grad = dot(gu_v[pl.ds(k * rows, rows)], w_v[at], 1, 1)
            p[k, :, at] = grad.astype(BF16)
            return c

        lax.fori_loop(0, width // tile, piece, 0)

    def meanwhile():
        for k, part in enumerate((b0, b1, b2, b3)):

            def piece(j, c):
                at = pl.ds(pl.multiple_of(j * tile, tile), tile)
                grad = dot(hidden[pl.ds(k * rows, rows)], w_d[at], 1, 1)
                part[:, at] = grad.astype(BF16)
                return c

            lax.fori_loop(0, width // tile, piece, 0)

    def finish(r, total):
        d_z = d_out[r].astype(F32) + norm_back(z[r], gain[...], total)
        dz_o[r] = d_z
        return d_z

    sum_and_gather(produce, finish, dz_all, scratch, meanwhile)


def mlp_back(d_g, d_u, w_gu, hidden, w_d, z, d_out, gain):
    rows, width = z.shape
    vmem = pl.BlockSpec(memory_space=pltpu.VMEM)
    anywhere = pl.BlockSpec(memory_space=pl.ANY)
    part = jax.ShapeDtypeStruct((rows, width), BF16)
    return pl.pallas_call(
        mlp_back_body,
        out_shape=(
            jax.ShapeDtypeStruct((rows, width), F32),
            jax.ShapeDtypeStruct((4, rows, width), BF16),
        )
        + (part,) * 4,
        in_specs=[anywhere] * 3 + [vmem] * 5,
        out_specs=(vmem, anywhere) + (vmem,) * 4,
        scratch_shapes=[
            pltpu.VMEM((4 * rows, 2 * d_g.shape[1]), BF16),
            pltpu.VMEM(w_gu.shape, BF16),
            pltpu.SemaphoreType.DMA((8 + width // 256,)),
        ]
        + sum_scratch(rows, width),
        compiler_params=pltpu.CompilerParams(
            collective_id=2, has_side_effects=True, vmem_limit_bytes=60 * MIB
        ),
        name="mlp_back",
    )(d_g, d_u, w_gu, hidden, w_d, z, d_out, gain)


def in_back_body(
    order,
    ay_s,
    w_t,
    gain,
    dz_s,
    x_s,
    z_s,
    s0,
    s1,
    s2,
    s3,
    gu_s,
    o_s,
    o,
    block_o,
    gu_p,
    o_p,
    w_xy,
    d_ay,
    d_z,
    x,
    z,
    b0,
    b1,
    b2,
    b3,
    load_sem,
    *scratch,
):
    own_sem, send_sem, recv_sem = scratch[7:]
    p, from_one, from_two = scratch[0], scratch[5], scratch[6]
    rows, width = x.shape
    tile, step = 256, 16

    def load_rows(k):
        at = pl.ds(k * rows, rows)
        return pltpu.make_async_copy(ay_s.at[at], d_ay.at[at], load_sem.at[k])

    def load_tile(j):
        at = pl.ds(pl.multiple_of(j * tile, tile), tile)
        src = w_t.at[at, pl.ds(0, w_xy.shape[1])]
        return pltpu.make_async_copy(src, w_xy.at[at], load_sem.at[4 + j])

    load_rows(3).start()
    for j in range(width // tile):
        load_tile(j).start()
    for k in (1, 2, 0):
        load_rows(k).start()
    pairs = ((z_s, z), (s0, b0), (s1, b1), (s2, b2), (s3, b3), (dz_s, d_z), (x_s, x))
    later = [
        pltpu.make_async_copy(src, to, load_sem.at[4 + width // tile + j])
        for j, (src, to) in enumerate(pairs)
    ]
    for copy in later:
        copy.start()
    one, two = dp_peers()
    meet(dp_others())
    send = dp_sender(send_sem, recv_sem)
    size = width // len(order)
    owned = []

    def outward(v):
        return jnp.concatenate([v[:, b * size : (b + 1) * size] for b in order], axis=1)

    def produce(k):
        load_rows(k).wait()

        def piece(j, c):
            if k == 3:
                load_tile(j).wait()
            at = pl.ds(pl.multiple_of(j * tile, tile), tile)
            grad = dot(d_ay[pl.ds(k * rows, rows)], w_xy[at], 1, 1)
            p[k, :, at] = grad.astype(BF16)
            return c

        lax.fori_loop(0, width // tile, piece, 0)

    def block_out(k, c):
        r = pl.ds(pl.multiple_of(k * step, step), step)
        total = z[r]
        for part in (b0, b1, b2, b3):
            total = total + part[r].astype(F32)
        block_o[r] = outward(total).astype(BF16)
        return c

    def meanwhile():
        pairs = [(gu_s, gu_p), (o_s, o_p)]
        owned.extend(owners_start(starter(send_sem, recv_sem), 6, pairs, own_sem))
        for copy in later:
            copy.wait()
        lax.fori_loop(0, rows // step, block_out, 0)

    copies = sum_over(send, scratch[:7], one, two, produce, meanwhile)

    def rows_of(k, c):
        r = pl.ds(pl.multiple_of(k * step, step), step)
        total = p[0, r].astype(F32) + from_one[r].astype(F32) + from_two[r].astype(F32)
        o[r] = outward(d_z[r] + norm_back(x[r].astype(F32), gain[...], total)).astype(BF16)
        return c

    lax.fori_loop(0, rows // step, rows_of, 0)
    for copy in copies:
        copy.wait_send()
    for copy in owned:
        copy.wait()


def in_back(d_ay, w_t, d_z, x, gain, z, parts, order, gu_s, o_s):
    rows, width = x.shape
    depth = gu_s.shape[0] // 4
    vmem = pl.BlockSpec(memory_space=pltpu.VMEM)
    anywhere = pl.BlockSpec(memory_space=pl.ANY)
    scratch = sum_scratch(rows, width)
    return pl.pallas_call(
        functools.partial(in_back_body, order),
        out_shape=(
            jax.ShapeDtypeStruct((rows, width), BF16),
            jax.ShapeDtypeStruct((rows, width), BF16),
            jax.ShapeDtypeStruct((4, depth, gu_s.shape[1]), BF16),
            jax.ShapeDtypeStruct((4, depth, o_s.shape[1]), BF16),
        ),
        in_specs=[anywhere] * 2 + [vmem] + [anywhere] * 9,
        out_specs=(vmem, vmem, anywhere, anywhere),
        scratch_shapes=[
            pltpu.VMEM((width, d_ay.shape[1]), BF16),
            pltpu.VMEM(d_ay.shape, BF16),
            pltpu.VMEM((rows, width), F32),
            pltpu.VMEM((rows, width), BF16),
            pltpu.VMEM((rows, width), F32),
        ]
        + [pltpu.VMEM((rows, width), BF16)] * 4
        + [pltpu.SemaphoreType.DMA((11 + width // 256,))]
        + scratch[:7]
        + [
            pltpu.SemaphoreType.DMA((2,)),
            pltpu.SemaphoreType.DMA((12,)),
            pltpu.SemaphoreType.DMA((12,)),
        ],
        compiler_params=pltpu.CompilerParams(
            collective_id=8, has_side_effects=True, vmem_limit_bytes=60 * MIB
        ),
        name="in_back",
    )(d_ay, w_t, gain, d_z, x, z, *parts, gu_s, o_s)


def in_grads_body(n, d_ay, side, o):
    width = d_ay.shape[1]
    o[:, :width] = dot(n[...], d_ay[...], 0, 0).astype(BF16)
    o[:, width:] = side[...].astype(BF16)


def in_grads(n, d_ay, side):
    rows, wide = n.shape
    width = d_ay.shape[1]
    tile = 256
    return pl.pallas_call(
        in_grads_body,
        grid=(wide // tile,),
        out_shape=jax.ShapeDtypeStruct((wide, width + side.shape[1]), BF16),
        in_specs=[
            pl.BlockSpec((rows, tile), lambda j: (0, j)),
            pl.BlockSpec((rows, width), lambda j: (0, 0)),
            pl.BlockSpec((tile, side.shape[1]), lambda j: (j, 0)),
        ],
        out_specs=pl.BlockSpec((tile, width + side.shape[1]), lambda j: (j, 0)),
        compiler_params=pltpu.CompilerParams(vmem_limit_bytes=60 * MIB),
        name="in_grads",
    )(n, d_ay, side)


def sigmoid(x):
    return 1.0 / (1.0 + jnp.exp(-x))


def softplus(x):
    e = jnp.exp(-jnp.abs(x))
    ratio = e / (2.0 + e)
    square = ratio * ratio
    series = jnp.full_like(x, 1.0 / 13.0)
    for k in (11, 9, 7, 5, 3, 1):
        series = 1.0 / k + square * series
    return jnp.maximum(x, 0.0) + 2.0 * ratio * series


def input_scale(la, decay):
    x = 2.0 * la
    series = 1.0 + x * (1.0 / 6.0)
    for k in range(5, 1, -1):
        series = 1.0 + x * (1.0 / k) * series
    return jnp.sqrt(jnp.where(x > -0.125, -x * series, 1.0 - decay * decay))


def group_scan(decay, value, backwards):
    rows, width = decay.shape
    decay = decay.reshape(rows // 8, 8, width)
    value = value.reshape(rows // 8, 8, width)
    row = lax.broadcasted_iota(jnp.int32, decay.shape, 1)
    for k in (1, 2, 4):
        shift = 8 - k if backwards else k
        inside = row < 8 - k if backwards else row >= k
        near_value = jnp.where(inside, pltpu.roll(value, shift, 1), 0.0)
        near_decay = jnp.where(inside, pltpu.roll(decay, shift, 1), 1.0)
        value = value + decay * near_value
        decay = decay * near_decay
    return decay.reshape(rows, width), value.reshape(rows, width)


def chain_ends(decays, states, first, groups, backwards, carry):
    total = jnp.ones_like(carry)
    for k in reversed(range(groups)) if backwards else range(groups):
        at = pl.ds(first + 8 * k + (0 if backwards else 7), 1)
        decay = decays[at]
        carry = states[at] + decay * carry
        total = total * decay
    return total, carry


def chain_states(decays, states, first, groups, backwards, carry):
    for k in reversed(range(groups)) if backwards else range(groups):
        at = pl.ds(pl.multiple_of(first + 8 * k, 8), 8)
        state = states[at] + decays[at] * carry
        states[at] = state
        carry = state[0:1] if backwards else state[7:8]


def seq_exchange(count, src, slots, send_sem, recv_sem):
    dp, me = lax.axis_index("dp"), lax.axis_index("seq")
    copies = []
    for j in range(1, count):
        copy = pltpu.make_async_remote_copy(
            src,
            slots.at[me],
            send_sem.at[j],
            recv_sem.at[j],
            device_id=(dp, (me + j) % count),
            device_id_type=MESH,
        )
        copy.start()
        copies.append(copy)
    for copy in copies:
        copy.wait()


def states_body(
    count,
    used,
    order,
    n,
    w_t,
    mix,
    vec,
    cot,
    valid,
    a,
    y_o,
    xc_o,
    la_o,
    h_o,
    hin_o,
    ends_o,
    rim_o,
    own,
    own_all,
    pad,
    decays,
    mine,
    rim_mine,
    w_xy,
    own_sem,
    load_sem,
    send_sem,
    recv_sem,
):
    load = pltpu.make_async_copy(w_t.at[:, pl.ds(0, 2 * used)], w_xy, load_sem)
    load.start()
    dp, me = lax.axis_index("dp"), lax.axis_index("seq")
    seqs, span, width = a.shape
    groups = span // 8
    one, two = dp_peers()
    meet([(one, me), (two, me)] + [(dp, (me + j) % count) for j in range(1, count)])
    send = dp_sender(send_sem, recv_sem)
    step, part = 32, own.shape[1] // len(order)

    def place(k, c):
        r = pl.ds(pl.multiple_of(k * step, step), step)
        v = jnp.where(valid[r] > 0.0, cot[r].astype(F32), 0.0).astype(BF16)
        own[r] = jnp.concatenate([v[:, b * part : (b + 1) * part] for b in order], axis=1)
        return c

    lax.fori_loop(0, own.shape[0] // step, place, 0)
    near = gather_start(send, count, own, own_all, one, two)
    keep = pltpu.make_async_copy(own, own_all.at[0], own_sem)
    keep.start()
    load.wait()
    spare = jnp.zeros((span, width - used), F32)

    def project(s, c):
        rows = pl.ds(pl.multiple_of(s * span, span), span)
        both = dot(n[rows], w_xy[...])
        a[s] = jnp.concatenate([both[:, :used], spare], axis=1).astype(BF16)
        y_o[rows] = jnp.concatenate([both[:, used:], spare], axis=1)
        return c

    last = [n[s * span + span - 16 : (s + 1) * span] for s in range(seqs)]
    edge = dot(jnp.concatenate(last, axis=0), w_xy[:, 0:width])
    column = lax.broadcasted_iota(jnp.int32, edge.shape, 1)
    edge = jnp.where(column < used, edge, 0.0).astype(BF16)
    for s in range(seqs):
        rim_mine[s] = edge[s * 16 : (s + 1) * 16]
    rim = pltpu.make_async_remote_copy(
        rim_mine,
        rim_o,
        send_sem.at[0],
        recv_sem.at[0],
        device_id=(dp, (me + 1) % count),
        device_id_type=MESH,
    )
    rim.start()
    project(0, 0)
    rim.wait()
    inside = jnp.where(me > 0, 1.0, 0.0)
    zero = jnp.zeros((1, width), F32)

    def local(s, c):
        first = pl.multiple_of(s * span, span)
        rows = pl.ds(first, span)
        pad[0:8] = rim_o[s, 8:16].astype(F32) * inside
        pad[8 : 8 + span] = a[s].astype(F32)
        conv = vec[4:5] + sum(vec[k : k + 1] * pad[8 - k : 8 - k + span] for k in range(4))
        xc = conv.astype(BF16)
        xc_o[s] = xc
        q = dot(xc, mix[...])
        r = sigmoid(q[:, :width] + vec[5:6])
        i = sigmoid(q[:, width:] + vec[6:7])
        la = vec[7:8] * r
        la_o[rows] = la
        decay = jnp.exp(la)
        drive = input_scale(la, decay) * (i * xc.astype(F32))
        decays[rows], h_o[rows] = group_scan(decay, drive, False)
        total, state = chain_ends(decays, h_o, first, groups, False, zero)
        mine[0, pl.ds(s, 1)] = total
        mine[1, pl.ds(s, 1)] = state
        return c

    def local_and_next(s, c):
        local(s, c)
        return project(s + 1, c)

    lax.fori_loop(0, seqs - 1, local_and_next, 0)
    local(seqs - 1, 0)
    far = gather_forward(send, count, near, own_all, one, two)
    ends_o[me] = mine[...]
    seq_exchange(count, mine, ends_o, send_sem, recv_sem)
    state = jnp.zeros((seqs, width), F32)
    for p in range(count - 1):
        state = jnp.where(p < me, ends_o[p, 0] * state + ends_o[p, 1], state)
    hin_o[...] = state

    def states(s, c):
        first = pl.multiple_of(s * span, span)
        chain_states(decays, h_o, first, groups, False, hin_o[pl.ds(s, 1)])
        return c

    lax.fori_loop(0, seqs, states, 0)
    gather_wait(near, far)
    keep.wait()


def recurrent_states(n, w_t, mix, vec, cot, valid, seqs, used, order):
    count = lax.axis_size("seq")
    rows, wide = n.shape
    span, width = rows // seqs, mix.shape[0]
    vmem = pl.BlockSpec(memory_space=pltpu.VMEM)
    anywhere = pl.BlockSpec(memory_space=pl.ANY)
    return pl.pallas_call(
        functools.partial(states_body, count, used, order),
        out_shape=(
            jax.ShapeDtypeStruct((seqs, span, width), BF16),
            jax.ShapeDtypeStruct((rows, width), F32),
            jax.ShapeDtypeStruct((seqs, span, width), BF16),
            jax.ShapeDtypeStruct((rows, width), F32),
            jax.ShapeDtypeStruct((rows, width), F32),
            jax.ShapeDtypeStruct((seqs, width), F32),
            jax.ShapeDtypeStruct((count, 2, seqs, width), F32),
            jax.ShapeDtypeStruct((seqs, 16, width), BF16),
            jax.ShapeDtypeStruct(cot.shape, BF16),
            jax.ShapeDtypeStruct((4,) + cot.shape, BF16),
        ),
        in_specs=[vmem, anywhere] + [vmem] * 4,
        out_specs=(vmem,) * 9 + (anywhere,),
        scratch_shapes=[
            pltpu.VMEM((span + 8, width), F32),
            pltpu.VMEM((rows, width), F32),
            pltpu.VMEM((2, seqs, width), F32),
            pltpu.VMEM((seqs, 16, width), BF16),
            pltpu.VMEM((wide, 2 * used), BF16),
            pltpu.SemaphoreType.DMA,
            pltpu.SemaphoreType.DMA,
            pltpu.SemaphoreType.DMA((count + 6,)),
            pltpu.SemaphoreType.DMA((count + 6,)),
        ],
        compiler_params=pltpu.CompilerParams(
            collective_id=4, has_side_effects=True, vmem_limit_bytes=60 * MIB
        ),
        name="recurrent_states",
    )(n, w_t, mix, vec, cot, valid)


def side_places(share, size, block):
    rest, narrow = size - LANES, 32
    kept = min(share, block - 2 * share)
    lanes = LANES - narrow
    assert 0 < 2 * rest <= lanes
    places = [(k, 0, share, 0, LANES, k * share, 0) for k in range(2)]
    places += [(k, 0, kept, LANES, size, 2 * share, k * rest) for k in range(2)]
    row = 2 * share
    for k in range(2):
        for first in range(LANES, size, narrow):
            if kept < share:
                places.append((k, kept, share, first, min(first + narrow, size), row, lanes))
                row += share - kept
    for first in range(0, share, narrow):
        places.append((2, 0, 8, first, min(first + narrow, share), row, lanes))
        row += 8
    assert row <= block
    return places


def side_read(side, share, size, which):
    wanted = [p for p in side_places(share, size, side.shape[0]) if p[0] == which]
    tops = sorted({p[1] for p in wanted if p[3] >= LANES or which == 2})

    def piece(p):
        return side[p[5] : p[5] + p[2] - p[1], p[6] : p[6] + p[4] - p[3]]

    rows = []
    for top in tops:
        parts = [piece(p) for p in wanted if p[1] == top and (p[3] >= LANES or which == 2)]
        rows.append(parts[0] if len(parts) == 1 else jnp.concatenate(parts, axis=1))
    value = rows[0] if len(rows) == 1 else jnp.concatenate(rows, axis=0)
    if which == 2:
        return value
    return jnp.concatenate([piece(wanted[0]), value], axis=1)


def back_body(
    count,
    nb,
    size,
    dz_s,
    w_t,
    y_s,
    h_s,
    la_s,
    xc,
    a,
    rim,
    mix,
    vec,
    h_in,
    ends,
    lam,
    d_s,
    day_o,
    side_o,
    d_p,
    dz,
    y,
    h,
    la_all,
    w_o,
    gate_sum,
    sums,
    dq_all,
    grad,
    decays,
    pad,
    dxc,
    after,
    mine,
    sent,
    row_sem,
    load_sem,
    own_sem,
    send_sem,
    recv_sem,
):
    moved = ((dz_s, dz), (y_s, y), (h_s, h), (la_s, la_all))

    def load_rows(s, j):
        at = pl.ds(pl.multiple_of(s * xc.shape[1], xc.shape[1]), xc.shape[1])
        return pltpu.make_async_copy(moved[j][0].at[at], moved[j][1].at[at], row_sem.at[j, s])

    for j in range(4):
        load_rows(0, j).start()
    load = pltpu.make_async_copy(w_t.at[:, pl.ds(2 * nb * size, xc.shape[2])], w_o, load_sem)
    load.start()
    for s in range(1, xc.shape[0]):
        for j in range(4):
            load_rows(s, j).start()
    dp, me = lax.axis_index("dp"), lax.axis_index("seq")
    seqs, span, width = xc.shape
    groups = span // 8
    meet(dp_others() + [(dp, (me + j) % count) for j in range(1, count)])
    used = nb * size
    owned = owners_start(starter(send_sem, recv_sem), count, [(d_s, d_p)], own_sem)
    sums[...] = jnp.zeros_like(sums)
    load.wait()

    zero = jnp.zeros((1, width), F32)

    def outer(s, c):
        first = pl.multiple_of(s * span, span)
        rows = pl.ds(first, span)
        for j in range(4):
            load_rows(s, j).wait()
        d_o = dot(dz[rows], w_o[...])
        v = y[rows]
        square = v * v
        t = jnp.tanh(GELU_SCALE * v * (1.0 + GELU_CUBE * square))
        act = 0.5 * v * (1.0 + t)
        slope = 0.5 * (1.0 + t) + 0.5 * v * (1.0 - t * t) * (
            GELU_SCALE * (1.0 + 3.0 * GELU_CUBE * square)
        )
        day_o[rows, used : 2 * used] = (d_o * h[rows] * slope)[:, :used].astype(BF16)
        decay = jnp.exp(la_all[rows])
        pad[0:span] = decay
        pad[span : span + 1] = jnp.ones((1, width), F32)
        decays[rows], grad[rows] = group_scan(pad[1 : span + 1], d_o * act, True)
        _, state = chain_ends(decays, grad, first, groups, True, zero)
        mine[pl.ds(s, 1)] = decay[0:1] * state
        return c

    lax.fori_loop(0, seqs, outer, 0)
    sent[me] = mine[...]
    seq_exchange(count, mine, sent, send_sem, recv_sem)
    state = jnp.zeros((seqs, width), F32)
    for p in range(count - 1, 0, -1):
        state = jnp.where(p > me, ends[p, 0] * state + sent[p], state)
    mine[...] = state

    def states(s, c):
        first = pl.multiple_of(s * span, span)
        chain_states(decays, grad, first, groups, True, mine[pl.ds(s, 1)])
        return c

    lax.fori_loop(0, seqs, states, 0)

    def gates(s, c):
        rows = pl.ds(pl.multiple_of(s * span, span), span)
        g = grad[rows]
        la = la_all[rows]
        decay = jnp.exp(la)
        pad[7:8] = h_in[pl.ds(s, 1)]
        pad[8 : 8 + span] = h[rows]
        h_prev = pad[7 : 7 + span]
        xc_b = xc[s]
        xcf = xc_b.astype(F32)
        q = dot(xc_b, mix[...])
        r = sigmoid(q[:, :width] + vec[5:6])
        i = sigmoid(q[:, width:] + vec[6:7])
        beta = input_scale(la, decay)
        gi = g * i
        dla = decay * (g * h_prev - gi * xcf * (decay / beta))
        dq_r = dla * la * (1.0 - r)
        gib = gi * beta
        dq_i = gib * xcf * (1.0 - i)
        sums[5:6] += jnp.sum(dq_r, axis=0, keepdims=True)
        sums[6:7] += jnp.sum(dq_i, axis=0, keepdims=True)
        sums[7:8] += jnp.sum(dla * r, axis=0, keepdims=True)
        dq = jnp.concatenate([dq_r.astype(BF16), dq_i.astype(BF16)], axis=1)
        dq_all[rows] = dq
        dxc[s] = (gib + dot(dq, mix[...], 1, 1)).astype(BF16)
        return c

    lax.fori_loop(0, seqs, gates, 0)
    copy = pltpu.make_async_remote_copy(
        dxc.at[:, pl.ds(0, 16)],
        after,
        send_sem.at[0],
        recv_sem.at[0],
        device_id=(dp, (me + count - 1) % count),
        device_id_type=MESH,
    )
    copy.start()
    for b in range(nb):
        x_b = xc[:, :, b * size : (b + 1) * size].reshape(seqs * span, size)
        for k in range(2):
            dq_b = dq_all[:, k * width + b * size : k * width + (b + 1) * size]
            gate_sum[k, b * size : (b + 1) * size] = dot(x_b, dq_b, 0, 0)
    copy.wait()
    inside = jnp.where(me > 0, 1.0, 0.0)
    going_on = jnp.where(me < count - 1, 1.0, 0.0)

    def conv(s, c):
        rows = pl.ds(pl.multiple_of(s * span, span), span)
        d = dxc[s].astype(F32)
        pad[0:span] = d
        pad[span : span + 8] = after[s, 0:8].astype(F32) * going_on
        d_a = sum(vec[k : k + 1] * pad[k : k + span] for k in range(4))
        day_o[rows, 0:used] = d_a[:, :used].astype(BF16)
        pad[0:8] = rim[s, 8:16].astype(F32) * inside
        pad[8 : 8 + span] = a[s].astype(F32)
        for k in range(4):
            sums[k : k + 1] += jnp.sum(d * pad[8 - k : 8 - k + span], axis=0, keepdims=True)
        sums[4:5] += jnp.sum(d, axis=0, keepdims=True)
        return c

    lax.fori_loop(0, seqs, conv, 0)
    sums[7:8] = sums[7:8] * (-GATE_SCALE * sigmoid(lam[0:1]))

    share = used // count
    block = side_o.shape[0] // count
    side_o[...] = jnp.zeros_like(side_o)
    for p in range(count):
        for which, top, bottom, left, right, row, lane in side_places(share, size, block):
            at = p * block + row
            if which == 2:
                piece = sums[:, p * share + left : p * share + right]
            else:
                piece = gate_sum[which, p * share + top : p * share + bottom, left:right]
            side_o[at : at + bottom - top, lane : lane + right - left] = piece
    for copy in owned:
        copy.wait()


def recurrent_back(dz, w_t, y, h, la, xc, a, rim, mix, vec, h_in, ends, lam, d_s, nb, size, side):
    count = lax.axis_size("seq")
    seqs, span, width = xc.shape
    rows = seqs * span
    anywhere = pl.BlockSpec(memory_space=pl.ANY)
    vmem = pl.BlockSpec(memory_space=pltpu.VMEM)
    return pl.pallas_call(
        functools.partial(back_body, count, nb, size),
        out_shape=(
            jax.ShapeDtypeStruct((rows, 2 * nb * size), BF16),
            jax.ShapeDtypeStruct(side, F32),
            jax.ShapeDtypeStruct((4, d_s.shape[0] // 4, d_s.shape[1]), BF16),
        ),
        in_specs=[anywhere] * 5 + [vmem] * 8 + [anywhere],
        out_specs=(vmem,) * 2 + (anywhere,),
        scratch_shapes=[
            pltpu.VMEM(dz.shape, BF16),
            pltpu.VMEM((rows, width), F32),
            pltpu.VMEM((rows, width), F32),
            pltpu.VMEM((rows, width), F32),
            pltpu.VMEM((dz.shape[1], width), BF16),
            pltpu.VMEM((2, nb * size, size), F32),
            pltpu.VMEM((8, width), F32),
            pltpu.VMEM((rows, 2 * width), BF16),
            pltpu.VMEM((rows, width), F32),
            pltpu.VMEM((rows, width), F32),
            pltpu.VMEM((span + 8, width), F32),
            pltpu.VMEM((seqs, span, width), BF16),
            pltpu.VMEM((seqs, 16, width), BF16),
            pltpu.VMEM((seqs, width), F32),
            pltpu.VMEM((count, seqs, width), F32),
            pltpu.SemaphoreType.DMA((4, seqs)),
            pltpu.SemaphoreType.DMA,
            pltpu.SemaphoreType.DMA((1,)),
            pltpu.SemaphoreType.DMA((count + 3,)),
            pltpu.SemaphoreType.DMA((count + 3,)),
        ],
        compiler_params=pltpu.CompilerParams(
            collective_id=5, has_side_effects=True, vmem_limit_bytes=60 * MIB
        ),
        name="recurrent_back",
    )(dz, w_t, y, h, la, xc, a, rim, mix, vec, h_in, ends, lam, d_s)


def gelu_parts(v):
    square = v * v
    t = jnp.tanh(GELU_SCALE * v * (1.0 + GELU_CUBE * square))
    half = 0.5 * (1.0 + t)
    slope = half + 0.5 * v * (1.0 - t * t) * (GELU_SCALE * (1.0 + 3.0 * GELU_CUBE * square))
    return v * half, slope


def up_body(n, w_g, w_u, hidden_o, act_o, slope_o):
    step = n.shape[0] // 8
    for k in range(8):
        r = slice(k * step, (k + 1) * step)
        g, up = dot(n[r], w_g[...]), dot(n[r], w_u[...])
        act, slope = gelu_parts(g)
        hidden_o[r] = (act * up).astype(BF16)
        act_o[r] = act.astype(BF16)
        slope_o[r] = (slope * up).astype(BF16)


def mlp_up(n, w_gu):
    rows, width = n.shape
    cols = w_gu.shape[1] // 2
    tile = 768
    count = cols // tile
    out = pl.BlockSpec((rows, tile), lambda j: (0, j))
    return pl.pallas_call(
        up_body,
        grid=(count,),
        out_shape=(jax.ShapeDtypeStruct((rows, cols), BF16),) * 3,
        in_specs=[
            pl.BlockSpec((rows, width), lambda j: (0, 0)),
            pl.BlockSpec((width, tile), lambda j: (0, j)),
            pl.BlockSpec((width, tile), lambda j: (0, j + count)),
        ],
        out_specs=(out,) * 3,
        compiler_params=pltpu.CompilerParams(vmem_limit_bytes=60 * MIB),
        name="mlp_up",
    )(n, w_gu, w_gu)


def down_body(d, w, slope, act, g_o, u_o):
    step = d.shape[0] // 4
    for k in range(4):
        r = slice(k * step, (k + 1) * step)
        grad = dot(d[r], w[...])
        g_o[r] = (grad * slope[r].astype(F32)).astype(BF16)
        u_o[r] = (grad * act[r].astype(F32)).astype(BF16)


def mlp_down_back(d, w_d, slope, act):
    rows, width = d.shape
    cols = w_d.shape[1]
    tile = 512
    part = pl.BlockSpec((rows, tile), lambda j: (0, j))
    return pl.pallas_call(
        down_body,
        grid=(cols // tile,),
        out_shape=(jax.ShapeDtypeStruct((rows, cols), BF16),) * 2,
        in_specs=[
            pl.BlockSpec((rows, width), lambda j: (0, 0)),
            pl.BlockSpec((width, tile), lambda j: (0, j)),
            part,
            part,
        ],
        out_specs=(part, part),
        compiler_params=pltpu.CompilerParams(vmem_limit_bytes=60 * MIB),
        name="mlp_down_back",
    )(d, w_d, slope, act)


def weight_grads_body(n, *refs):
    grads, o = refs[:-1], refs[-1]
    first = 0
    for d in grads:
        width = d.shape[1]
        o[:, first : first + width] = dot(n[...], d[...], 0, 0).astype(BF16)
        first += width


def weight_grads(n, *grads):
    rows, wide = n.shape
    width = sum(d.shape[1] for d in grads)
    tile = 256
    return pl.pallas_call(
        weight_grads_body,
        grid=(wide // tile,),
        out_shape=jax.ShapeDtypeStruct((wide, width), BF16),
        in_specs=[pl.BlockSpec((rows, tile), lambda j: (0, j))]
        + [pl.BlockSpec(d.shape, lambda j: (0, 0)) for d in grads],
        out_specs=pl.BlockSpec((tile, width), lambda j: (j, 0)),
        compiler_params=pltpu.CompilerParams(vmem_limit_bytes=60 * MIB),
        name="weight_grads",
    )(n, *grads)


def weigh(w, parts, places):
    cols = w.shape[2] // 4
    squares = jnp.zeros((w.shape[1], 1), F32)
    along = jnp.zeros((w.shape[1], 1), F32)
    for k in range(3):
        part, first = parts[places[k][0]], places[k][1]
        for dp in range(4):
            grad = part[dp, :, first : first + cols].astype(F32)
            squares += jnp.sum(grad * grad, axis=1, keepdims=True)
            if k < 2:
                weight = w[k, :, dp * cols : (dp + 1) * cols].astype(BF16).astype(F32)
                along += jnp.sum(weight * grad, axis=1, keepdims=True)
    return squares, along


MLP_PLACES = ((0, 0), (0, 1), (1, 0))
TEMPORAL_PLACES = ((0, 0), (0, 1), (1, 0))


def finish_body(
    count,
    in_s,
    gu_p,
    d_p,
    o_p,
    gains,
    t,
    mlp_s,
    norm_o,
    gain_o,
    side_o,
    xy_o,
    mlp,
    grads,
    along_out,
    along_in,
    seq_in,
    dp_in,
    mine,
    part,
    load_sem,
    own_sem,
    send_sem,
    recv_sem,
):
    dp, me = lax.axis_index("dp"), lax.axis_index("seq")
    width = xy_o.shape[2]
    loads = [
        pltpu.make_async_copy(in_s, grads, load_sem.at[0]),
        pltpu.make_async_copy(mlp_s, mlp, load_sem.at[1]),
    ]
    for copy in loads:
        copy.start()
    along = [(dp, (me + j) % count) for j in range(1, count)]
    meet(dp_others() + along)
    send = starter(send_sem, recv_sem)

    loads[0].wait()
    rest = grads[...].astype(F32)
    rows = grads.shape[0]
    weights = t[...].astype(F32).reshape(rows, t.shape[2])[:, :width]
    products = jnp.sum(weights * rest[:, :width], axis=1, keepdims=True)
    along_out[...] = jnp.broadcast_to(products, (rows, LANES)).reshape(along_out.shape)
    copies = [
        send(3 + k, along_out.at[peer[0]], along_in.at[dp], peer)
        for k, peer in enumerate(dp_others())
    ]
    along_in[dp] = along_out[dp]
    owned = owners_start(send, 0, [(in_s, xy_o)], own_sem)
    side_o[...] = rest[:, width:]
    total = jnp.sum(rest * rest, axis=0, keepdims=True)
    total = jnp.sum(total, axis=1, keepdims=True)
    cols = d_p.shape[2]
    loads[1].wait()
    squares, mlp_along = weigh(mlp, (gu_p, d_p), tuple((j, k * cols) for j, k in MLP_PLACES))
    for k in range(4):
        o_k = o_p[k].astype(F32)
        squares += jnp.sum(o_k * o_k, axis=1, keepdims=True)
    for copy in copies:
        copy.wait()
    temporal_along = (along_in[0] + along_in[1]) + (along_in[2] + along_in[3])
    gain_one = temporal_along[:, 0:1] / gains[:, 0:1]
    gain_two = mlp_along / gains[:, 1:2]
    lane = lax.broadcasted_iota(jnp.int32, gain_o.shape, 1)
    gain_o[...] = jnp.where(lane == 0, gain_one, gain_two)
    squares = squares + gain_one * gain_one + gain_two * gain_two
    total = total + jnp.sum(squares, axis=0, keepdims=True)
    mine[...] = jnp.broadcast_to(total, mine.shape)

    seq_in[me] = mine[...]
    copies = [send(6 + j, mine, seq_in.at[me], peer) for j, peer in enumerate(along)]
    for copy in copies:
        copy.wait()
    total = seq_in[0]
    for p in range(1, count):
        total = total + seq_in[p]
    part[...] = total
    copies = [send(5 + count + j, part, dp_in.at[j], peer) for j, peer in enumerate(dp_others())]
    for copy in copies:
        copy.wait()
    total = (part[...] + dp_in[1]) + (dp_in[2] + dp_in[0])
    norm_o[...] = jnp.sqrt(total)
    for copy in owned:
        copy.wait()


def finish(in_s, gu_p, d_p, o_p, gains, t, mlp_w, width):
    count = lax.axis_size("seq")
    depth = o_p.shape[1]
    vmem = pl.BlockSpec(memory_space=pltpu.VMEM)
    anywhere = pl.BlockSpec(memory_space=pl.ANY)
    tile = (8, LANES)
    sems = 8 + count
    return pl.pallas_call(
        functools.partial(finish_body, count),
        out_shape=(
            jax.ShapeDtypeStruct(tile, F32),
            jax.ShapeDtypeStruct((depth, LANES), F32),
            jax.ShapeDtypeStruct((in_s.shape[0], in_s.shape[1] - width), F32),
            jax.ShapeDtypeStruct((4, depth, width), BF16),
        ),
        in_specs=[anywhere] + [vmem] * 5 + [anywhere],
        out_specs=(vmem,) * 4,
        scratch_shapes=[
            pltpu.VMEM(mlp_w.shape, F32),
            pltpu.VMEM(in_s.shape, BF16),
            pltpu.VMEM((4, depth, LANES), F32),
            pltpu.VMEM((4, depth, LANES), F32),
            pltpu.VMEM((count,) + tile, F32),
            pltpu.VMEM((3,) + tile, F32),
            pltpu.VMEM(tile, F32),
            pltpu.VMEM(tile, F32),
            pltpu.SemaphoreType.DMA((2,)),
            pltpu.SemaphoreType.DMA((1,)),
            pltpu.SemaphoreType.DMA((sems,)),
            pltpu.SemaphoreType.DMA((sems,)),
        ],
        compiler_params=pltpu.CompilerParams(
            collective_id=3, has_side_effects=True, vmem_limit_bytes=60 * MIB
        ),
        name="finish",
    )(in_s, gu_p, d_p, o_p, gains, t, mlp_w)


def adam_body(rate, gate_rate, norm, gu_p, d_p, xy_p, o_p, gains, side, *refs):
    big, little, handed, refs = refs[:6], refs[6:15], refs[15:17], refs[17:]
    outs, little_o, handed_o, norm_o = refs[:8], refs[8:20], refs[20:22], refs[22]
    norm_o[...] = norm[0:1, 0:1]
    for src, out in zip(handed, handed_o):
        out[...] = src[...]
    factor = (CLIP_LEVEL / jnp.maximum(norm[...], CLIP_LEVEL))[0:1, 0:1]

    def small(which, at, grad, step_rate, decay_rate):
        values = [ref[at] for ref in little[which : which + 3]]
        new = adam_update(*values, grad * factor, step_rate, decay_rate)
        first_out = which // 3 * 4
        for ref, value in zip(little_o[first_out : first_out + 4], new):
            ref[at] = value

    @pl.when(pl.program_id(0) == 0)
    def _():
        depth = gains.shape[0]
        row = lax.broadcasted_iota(jnp.int32, (depth, depth), 0)
        diagonal = row == lax.broadcasted_iota(jnp.int32, (depth, depth), 1)
        turned = [
            jnp.sum(jnp.where(diagonal, gains[:, k : k + 1], 0.0), axis=0, keepdims=True)
            for k in range(2)
        ]
        whole = (slice(None), slice(None))
        small(0, whole, jnp.concatenate(turned, axis=0), 1.0, 0.0)
        share, _, size = little[6].shape
        rest = side[...]
        small(3, whole, side_read(rest, share, size, 2), 2.0, 0.0)
        for k in range(2):
            grad = side_read(rest, share, size, k)
            small(6, (slice(None), k, slice(None)), grad, gate_rate, WEIGHT_DECAY)

    for state, new, parts, places in (
        (big[0:3], outs[0:4], (gu_p, d_p), MLP_PLACES),
        (big[3:6], outs[4:8], (xy_p, o_p), TEMPORAL_PLACES),
    ):
        cols = state[0].shape[2] // 4
        for k in range(3):
            part, at = parts[places[k][0]], places[k][1] * cols
            grad = [part[dp, :, at : at + cols].astype(F32) for dp in range(4)]
            grad = jnp.concatenate(grad, axis=1) * factor
            values = adam_update(*[ref[k] for ref in state], grad, rate, WEIGHT_DECAY)
            for ref, value in zip(new, values):
                ref[k] = value


def adam(norm, gu_p, d_p, xy_p, o_p, gains, side, mlp, temporal, little, handed, rate, gate_rate):
    depth = o_p.shape[1]
    step = 16

    def whole(v):
        return pl.BlockSpec(v.shape, lambda j: (0,) * v.ndim)

    def part(v):
        return pl.BlockSpec((v.shape[0], step, v.shape[2]), lambda j: (0, j, 0))

    shapes, specs = [], []
    for group, spec in ((mlp, part), (temporal, part), (little[0:3], whole), (little[3:6], whole), (little[6:9], whole)):
        shapes += [jax.ShapeDtypeStruct(group[0].shape, kind) for kind in (F32, F32, F32, BF16)]
        specs += [spec(group[0])] * 4
    rows = handed[0].shape[0] * step // depth
    passing = pl.BlockSpec((rows, handed[0].shape[1]), lambda j: (j, 0))
    shapes += [jax.ShapeDtypeStruct(v.shape, v.dtype) for v in handed]
    specs += [passing] * 2
    shapes.append(jax.ShapeDtypeStruct((1, 1), F32))
    specs.append(pl.BlockSpec((1, 1), lambda j: (0, 0)))
    return pl.pallas_call(
        functools.partial(adam_body, rate, gate_rate),
        grid=(depth // step,),
        out_shape=tuple(shapes),
        in_specs=[whole(norm), part(gu_p), part(d_p), part(xy_p), part(o_p), whole(gains), whole(side)]
        + [part(v) for v in tuple(mlp) + tuple(temporal)]
        + [whole(v) for v in little]
        + [passing] * 2,
        out_specs=tuple(specs),
        compiler_params=pltpu.CompilerParams(vmem_limit_bytes=60 * MIB),
        name="adam",
    )(norm, gu_p, d_p, xy_p, o_p, gains, side, *mlp, *temporal, *little, *handed)


def inverse_rms(values):
    return lax.rsqrt(jnp.mean(values * values, axis=-1, keepdims=True) + NORM_EPS)


def norm_back(values, gain, grad):
    inv = inverse_rms(values)
    unit = values * inv
    scaled = grad * gain
    return inv * (scaled - unit * jnp.mean(scaled * unit, axis=-1, keepdims=True))


def gelu(values):
    return jax.nn.gelu(values, approximate=True)


def adam_update(weight, first_moment, second, gradient, step_rate, decay_rate):
    first_new = BETA_ONE * first_moment + (1.0 - BETA_ONE) * gradient
    second_new = BETA_TWO * second + (1.0 - BETA_TWO) * gradient * gradient
    adam_step = (first_new * (1.0 / (1.0 - BETA_ONE**STEP))) / (
        jnp.sqrt(second_new * (1.0 / (1.0 - BETA_TWO**STEP))) + ADAM_EPS
    )
    weight_new = weight - step_rate * (adam_step + decay_rate * weight)
    return (weight_new, first_new, second_new, weight_new.astype(BF16))


def shards(
    tokens,
    cotangent,
    lengths,
    gain_master,
    gain_first,
    gain_second,
    vector_master,
    vector_first,
    vector_second,
    gate_master,
    gate_first,
    gate_second,
    temporal_master,
    temporal_first,
    temporal_second,
    mlp_master,
    mlp_first,
    mlp_second,
):
    nd, ns = lax.axis_size("dp"), lax.axis_size("seq")
    local_seqs, span, D = tokens.shape
    n = local_seqs * span
    seqs = nd * local_seqs
    Dl, _, R = temporal_master.shape
    FF = mlp_master.shape[2]
    Rp, Fp = R // nd, FF // nd
    Rq = -(-Rp // LANES) * LANES
    BS = R // NB
    nb = Rp // BS
    rows = nd * Dl

    to_inner = [dp * ns + s for s in range(ns) for dp in range(nd)]
    to_outer = [s * nd + dp for dp in range(nd) for s in range(ns)]

    def over_seq(v):
        return lax.all_gather(v.reshape(rows, v.shape[2]), "seq", axis=0, tiled=True)

    def to_owner_seq(v):
        return lax.psum_scatter(v, "seq", scatter_dimension=0, tiled=True)

    with jax.named_scope("inputs"):
        temporal_w = jnp.transpose(temporal_master, (1, 0, 2))
        mlp_w = jnp.transpose(mlp_master, (1, 0, 2))
        packed = -(-3 * Rp // LANES) * LANES
        gate_rows = gate_master.shape[0]
        gain_b = gain_master.astype(BF16)
        cols_t, gates, vecs, gains = temporal_front(
            temporal_w, packed, gate_master, vector_master, gain_master
        )
        w_t = over_seq(cols_t)
        cols_gu, cols_d, n1, mix, vec, lam, gains, x = front(
            mlp_w,
            tokens.reshape(n, D),
            gates,
            vecs,
            gains,
            gate_rows,
            BS,
            nb,
            Rq,
            to_inner,
        )
        w_gu = over_seq(cols_gu)
        w_d = over_seq(cols_d)

        positions = lax.axis_index("seq") * span + jnp.arange(span, dtype=jnp.int32)
        valid = (positions[None, :] < lengths[:, None]).astype(F32).reshape(n, 1)

    with jax.named_scope("recurrent"):
        a, y, xc, la, h, h_in, ends, rim, out_grad, out_grad_all = recurrent_states(
            n1, w_t, mix, vec, cotangent.reshape(n, D), valid, seqs, Rp, to_inner
        )
        out_grad_all = out_grad_all.reshape(nd * n, D)
        o, z, n2 = mid(span, 2 * Rp, h, y, w_t, x, gains[1:2])
        n2 = n2.reshape(nd * n, D)

    with jax.named_scope("mlp"):
        hidden, act, slope = mlp_up(n2, w_gu)

    with jax.named_scope("mlp_grads"):
        dw_d = weight_grads(out_grad_all, hidden)
        slope, out_grad_all, dw_d = lax.optimization_barrier((slope, out_grad_all, dw_d))
        dw_d = to_owner_seq(dw_d)
        d_g, d_u = mlp_down_back(out_grad_all, w_d, slope, act)
        dw_gu = weight_grads(n2, d_g, d_u)
        d_g, d_u, dw_gu = lax.optimization_barrier((d_g, d_u, dw_gu))
        dw_gu = to_owner_seq(dw_gu)

    with jax.named_scope("mlp_back"):
        d_z, d_z_all, *partial = mlp_back(
            d_g, d_u, w_gu, hidden, w_d, z, out_grad, gains[1:2]
        )
        d_z_all = d_z_all.reshape(nd * n, D)
        partial = [partial[0]] + [swap(partial[k], k) for k in (1, 2, 3)]

    with jax.named_scope("recurrent_back"):
        dw_o = weight_grads(d_z_all, o)
        d_z_all, dw_o = lax.optimization_barrier((d_z_all, dw_o))
        dw_o = to_owner_seq(dw_o)
        side_shape = (ns * rows, LANES)
        d_ay, d_side, d_parts = recurrent_back(
            d_z_all, w_t, y, h, la, xc, a, rim, mix, vec, h_in, ends, lam, dw_d, nb, BS, side_shape
        )
        d_ay, dw_gu, partial = lax.optimization_barrier((d_ay, dw_gu, partial))
        d_in = in_grads(n1, d_ay, d_side)
        d_ay, d_in, dw_o = lax.optimization_barrier((d_ay, d_in, dw_o))
        d_in = to_owner_seq(d_in)

    with jax.named_scope("outputs"):
        tokens_grad, block_out, gu_parts, o_parts = in_back(
            d_ay, w_t, d_z, x, gains[0:1], z, partial, to_outer, dw_gu, dw_o
        )

    with jax.named_scope("owners"):

        gain_columns = jnp.pad(gain_b.astype(F32).T, ((0, 0), (0, LANES - 2)), constant_values=1.0)
        def turned(*arrays):
            return [jnp.transpose(v, (1, 0, 2)) for v in arrays]

        little = (
            (gain_master, gain_first, gain_second)
            + (vector_master, vector_first, vector_second)
            + (gate_master, gate_first, gate_second)
        )
        norm_tile, gain_grads, side, xy_parts = finish(
            d_in, gu_parts, d_parts, o_parts, gain_columns, cols_t, mlp_w, 2 * Rp
        )
        updated = adam(
            norm_tile,
            gu_parts,
            d_parts,
            xy_parts,
            o_parts,
            gain_grads,
            side,
            turned(mlp_master, mlp_first, mlp_second),
            turned(temporal_master, temporal_first, temporal_second),
            little,
            (block_out, tokens_grad),
            D**-0.5,
            BS**-0.5,
        )
        block_out, tokens_grad = [v.reshape(local_seqs, span, D) for v in updated[20:22]]
        mlp_out, temporal_out = tuple(turned(*updated[:4])), tuple(turned(*updated[4:8]))
        gain_out, vector_out, gate_out = [tuple(updated[k : k + 4]) for k in (8, 12, 16)]
        grad_norm = updated[22].reshape(())
    return (
        (block_out, tokens_grad, grad_norm)
        + gain_out
        + vector_out
        + gate_out
        + temporal_out
        + mlp_out
    )


def solution(mesh):
    across = P("dp", "seq", None)
    columns = P(None, ("dp", "seq"))
    owners = P(("dp", "seq"), None, None)
    return jax.shard_map(
        shards,
        mesh=mesh,
        in_specs=(across, across, P("dp")) + (columns,) * 6 + (owners,) * 9,
        out_specs=(across, across, P()) + (columns,) * 8 + (owners,) * 12,
        check_vma=False,
    )
```
